512 devices in a mesh: seq: 8 (over z), chan: 16 (over y_hi, x, core), frame: 4 (over y_lo).
Axes of the slice: x: 4, y: 8 (y_hi: 2, y_lo: 4; y = y_hi * 4 + y_lo), z: 8, core: 2. Of those that a mesh axis runs over, the one named last changes fastest.
Arguments:
- token_qkv: bfloat16 [16, 8, 64, 3, 24, 128], P('chan', 'frame', 'seq'), may hold values from -8 to 8
- text_kv: bfloat16 [16, 256, 2, 24, 128], P('chan', 'seq'), may hold values from -6 to 6
- residual: bfloat16 [16, 8, 64, 3072], P('chan', 'frame', 'seq'), may hold values from -6 to 6
- query_gain: float32 [128], replicated, may hold values from 1.5 to 6
- key_gain: float32 [128], replicated, may hold values from 1.5 to 6
- out_weight: bfloat16 [24, 128, 3072], P('seq'), may hold values from -0.109375 to 0.109375
- res_gate: float32 [16, 3072], P('chan'), may hold values from 0.5 to 2
- mod_shift: float32 [16, 3072], P('chan'), may hold values from -3 to 3
- mod_scale: float32 [16, 3072], P('chan'), may hold values from -0.9 to 0.9
- final_weight: bfloat16 [64, 3072], replicated, may hold values from -0.109375 to 0.109375
- final_bias: float32 [64], replicated, may hold values from -1.5 to 1.5
- text_len: int32 [16], P('chan'), may hold values from 1 to 256, as said below
- video_frames: int32 [16], P('chan'), may hold values from 1 to 8, as said below
- in_weight: bfloat16 [27, 16, 512], P(None, None, 'chan'), may hold values from -0.3125 to 0.3125
- in_bias: float32 [512], P('chan'), may hold values from -1.5 to 1.5
- group_gain: float32 [512], P('chan'), may hold values from 0.1 to 1.9
- group_bias: float32 [512], P('chan'), may hold values from -1.5 to 1.5
- conv_weight: bfloat16 [27, 512, 512], P(None, None, 'chan'), may hold values from -0.0546875 to 0.0546875
- conv_bias: float32 [512], P('chan'), may hold values from -1.5 to 1.5
Outputs:
- decoded: bfloat16 [16, 8, 512, 256], P('seq', 'frame', 'chan')
The draws below stay inside these ranges and needn't reach their ends.
Inputs may be any that keep to these rules, and one draw needn't show every extreme that they name: Text tokens at or past text_len of their video are padding; some video uses all 256 slots and some only one. latent frames at or past video_frames of their video are padding for the keys; some video uses all 8 frames and some only one.
All inputs are finite; a program needn't handle non-finite values.
Results may differ from the reference program's by a relative error of at most 0.022.
Values may be sent and summed in bfloat16 or wider, within the bound.
No kernel may reach another device: no remote copies, remote signals or barrier semaphores. Data moves between devices by JAX's collectives and lax.ppermute only.
A program may use at most 128 MiB of HBM per device.

```python
import math
import jax
import jax.numpy as jnp
from jax import lax

D = 3072
HEADS = 24
HD = 128
TXT = 256
LCH = 16
DCH = 512
GROUPS = 32
PH = 4
PW = 16
PATCHES = 64
LH = 8
LW = 32
PV = 64
FRAMES = 8
VIDEOS = 16


def pinned_counts(key, upper):
    counts = jax.random.randint(key, (VIDEOS,), 1, upper + 1, dtype=jnp.int32)
    order = jax.random.permutation(jax.random.fold_in(key, 1), VIDEOS)
    positions = jnp.arange(VIDEOS, dtype=jnp.int32)
    counts = jnp.where(positions == order[0], upper, counts)
    return jnp.where(positions == order[1], 1, counts)


def draw_text_len(key, part):
    key = jax.random.fold_in(key, 14)
    return pinned_counts(key, TXT)


def draw_video_frames(key, part):
    key = jax.random.fold_in(key, 15)
    return pinned_counts(key, FRAMES)


def draw_query_gain(key, part):
    key = jax.random.fold_in(key, 12)
    values = jax.random.uniform(key, (HD,), jnp.float32, 1.5, 2.5)
    return values


def draw_key_gain(key, part):
    key = jax.random.fold_in(key, 13)
    values = jax.random.uniform(key, (HD,), jnp.float32, 1.5, 2.5)
    return values


def draw_token_qkv(key, part):
    key = jax.random.fold_in(key, 11)
    base_key = jax.random.fold_in(key, 1)
    shape = (VIDEOS, FRAMES, PATCHES, 3, HEADS, HD)
    values = jnp.clip(jax.random.normal(base_key, shape, jnp.float32), -6.0, 6.0)
    return values.astype(jnp.bfloat16)


def steps_of(own_key, shape, shards, smallest, high):
    def one(position, parts):
        draws = jax.random.uniform(jax.random.fold_in(jax.random.fold_in(own_key, 6), position), (parts,), jnp.float32, smallest / len(shards), high / len(shards))
        return jnp.repeat(jnp.exp(draws), shape[position] // parts).reshape((-1,) + (1,) * (len(shape) - position - 1))

    factor_of = one(*shards[0])
    for cut in shards[1:]:
        factor_of = factor_of * one(*cut)
    return factor_of


def noise(rng, shape, deviation, bound, split=(), kind=jnp.bfloat16):
    entries = jax.random.normal(rng, shape, jnp.float32) * deviation
    if len(split) > 0:
        entries = steps_of(rng, shape, split, -0.22, 0.18) * entries
    return jnp.clip(entries, min=-bound, max=bound).astype(kind)


def setup_inputs(seed: int = 0) -> dict:
    seeds = jax.random.split(jax.random.key(seed), 20)
    token_qkv = draw_token_qkv(jax.random.fold_in(seeds[19], 71), 0)
    text_kv = noise(seeds[1], (VIDEOS, TXT, 2, HEADS, HD), 1.0, 6.0, ((0, 16), (1, 8)))
    residual = noise(seeds[2], (VIDEOS, FRAMES, PATCHES, D), 1.0, 6.0, ((0, 16), (1, 4), (2, 8)))
    query_gain = draw_query_gain(jax.random.fold_in(seeds[19], 71), 0)
    key_gain = draw_key_gain(jax.random.fold_in(seeds[19], 71), 0)
    out_weight = noise(seeds[5], (HEADS, HD, D), D ** -0.5, 0.109375, ((0, 8),))
    res_gate = jnp.clip(0.5 + 1.5 * jax.random.uniform(seeds[6], (VIDEOS, D), jnp.float32) ** steps_of(seeds[6], (VIDEOS, D), ((0, 16),), -0.2, 0.2), 0.5, 2.0)
    mod_shift = noise(seeds[7], (VIDEOS, D), 0.5, 3.0, ((0, 16),), jnp.float32)
    mod_scale = noise(seeds[8], (VIDEOS, D), 0.3, 0.9, ((0, 16),), jnp.float32)
    final_weight = noise(seeds[9], (PV, D), D ** -0.5, 0.109375)
    final_bias = noise(seeds[10], (PV,), 0.3, 1.5, (), jnp.float32)
    text_len = draw_text_len(jax.random.fold_in(seeds[19], 71), 0)
    video_frames = draw_video_frames(jax.random.fold_in(seeds[19], 71), 0)
    in_weight = noise(seeds[13], (27, LCH, DCH), (27 * LCH) ** -0.5, 0.3125, ((2, 16),))
    in_bias = noise(seeds[14], (DCH,), 0.3, 1.5, ((0, 16),), jnp.float32)
    group_gain = jnp.clip(1.0 + 0.18 * jax.random.normal(seeds[15], (DCH,), jnp.float32), 0.1, 1.9)
    group_bias = noise(seeds[16], (DCH,), 0.3, 1.5, ((0, 16),), jnp.float32)
    conv_weight = noise(seeds[17], (27, DCH, DCH), (27 * DCH) ** -0.5, 0.0546875, ((2, 16),))
    conv_bias = noise(seeds[18], (DCH,), 0.3, 1.5, ((0, 16),), jnp.float32)
    return dict(token_qkv=token_qkv, text_kv=text_kv, residual=residual, query_gain=query_gain, key_gain=key_gain, out_weight=out_weight, res_gate=res_gate, mod_shift=mod_shift, mod_scale=mod_scale, final_weight=final_weight, final_bias=final_bias, text_len=text_len, video_frames=video_frames, in_weight=in_weight, in_bias=in_bias, group_gain=group_gain, group_bias=group_bias, conv_weight=conv_weight, conv_bias=conv_bias)


EPSILON = 1e-06

def rms_scale(values, row_gain):
    values = values.astype(jnp.float32)
    mean_square = lax.optimization_barrier(jnp.mean(values * values, axis=-1, keepdims=True))
    return values * lax.rsqrt(mean_square + EPSILON) * row_gain

def conv_taps(running, volume, weight, frames_out):
    channels = volume.shape[0]
    height = volume.shape[3]
    breadth = volume.shape[4]
    padded = jnp.pad(volume, ((0, 0), (0, 0), (0, 0), (1, 1), (1, 1)))
    for tap_index in range(27):
        step_t = tap_index // 9
        step_y = tap_index // 3 % 3
        step_x = tap_index % 3
        window = padded[:, :, step_t:step_t + frames_out, step_y:step_y + height, step_x:step_x + breadth]
        running = running + lax.dot_general(weight[tap_index], window.reshape(channels, -1), (((0,), (0,)), ((), ())), preferred_element_type=jnp.float32)
    return running

def causal_front(volume):
    lead_frame = volume[:, :, :1]
    return jnp.concatenate([lead_frame, lead_frame, volume], axis=2)

def reference(token_qkv, text_kv, residual, query_gain, key_gain, out_weight, res_gate, mod_shift, mod_scale, final_weight, final_bias, text_len, video_frames, in_weight, in_bias, group_gain, group_bias, conv_weight, conv_bias):
    video_ids = jnp.arange(VIDEOS, dtype=jnp.int32)

    def one_video(video_id):
        token_mix = token_qkv[video_id].reshape(FRAMES * PATCHES, 3, HEADS, HD)
        text_part = text_kv[video_id]
        query_rows = rms_scale(token_mix[:, 0], query_gain).astype(jnp.bfloat16)
        key_video = rms_scale(token_mix[:, 1], key_gain).astype(jnp.bfloat16)
        key_text = rms_scale(text_part[:, 0], key_gain).astype(jnp.bfloat16)
        key_rows = jnp.concatenate([key_video, key_text], axis=0)
        value_rows = jnp.concatenate([token_mix[:, 2], text_part[:, 1]], axis=0)
        scores = jnp.einsum('qhd,khd->hqk', query_rows.astype(jnp.float32), key_rows.astype(jnp.float32)) / math.sqrt(HD)
        video_live = jnp.arange(FRAMES * PATCHES, dtype=jnp.int32) // PATCHES < video_frames[video_id]
        text_live = jnp.arange(TXT, dtype=jnp.int32) < text_len[video_id]
        live_keys = jnp.concatenate([video_live, text_live])
        scores = jnp.where(live_keys[None, None, :], scores, -jnp.inf)
        top_score = lax.optimization_barrier(jnp.max(scores, axis=-1, keepdims=True))
        raw_weights = jnp.exp(scores - top_score)
        weight_sum = lax.optimization_barrier(jnp.sum(raw_weights, axis=-1))
        prob_rows = raw_weights.astype(jnp.bfloat16)
        attended = jnp.einsum('hqk,khd->qhd', prob_rows.astype(jnp.float32), value_rows.astype(jnp.float32))
        attended = attended / jnp.transpose(weight_sum)[:, :, None]
        attended = attended.astype(jnp.bfloat16).reshape(FRAMES * PATCHES, D)
        projected = jnp.dot(attended, out_weight.reshape(D, D), preferred_element_type=jnp.float32)
        block_sum = residual[video_id].reshape(FRAMES * PATCHES, D).astype(jnp.float32) + res_gate[video_id] * projected
        centred = block_sum - lax.optimization_barrier(jnp.mean(block_sum, axis=-1, keepdims=True))
        variance = lax.optimization_barrier(jnp.mean(centred * centred, axis=-1, keepdims=True))
        normed = centred * lax.rsqrt(variance + EPSILON)
        modulated = (normed * (1.0 + mod_scale[video_id]) + mod_shift[video_id]).astype(jnp.bfloat16)
        latent = lax.dot_general(modulated, final_weight, (((1,), (1,)), ((), ())), preferred_element_type=jnp.float32)
        latent = (latent + final_bias).astype(jnp.bfloat16)
        latent = latent.reshape(FRAMES, PH, PW, LCH, 2, 2).transpose(3, 0, 1, 4, 2, 5).reshape(LCH, 1, FRAMES, LH, LW)
        start_zero = jnp.zeros((DCH, FRAMES * LH * LW), jnp.float32)
        hidden = (conv_taps(start_zero, causal_front(latent), in_weight, FRAMES) + in_bias[:, None]).astype(jnp.bfloat16)
        group_view = hidden.astype(jnp.float32).reshape(GROUPS, DCH // GROUPS, FRAMES, LH * LW)
        group_mean = lax.optimization_barrier(jnp.mean(group_view, axis=(1, 3), keepdims=True))
        group_var = lax.optimization_barrier(jnp.mean(group_view * group_view, axis=(1, 3), keepdims=True)) - group_mean * group_mean
        normed_groups = ((group_view - group_mean) * lax.rsqrt(group_var + EPSILON)).reshape(DCH, FRAMES * LH * LW)
        activated = jax.nn.silu(normed_groups * group_gain[:, None] + group_bias[:, None]).astype(jnp.bfloat16)
        activated = activated.reshape(DCH, 1, FRAMES, LH, LW)
        branch = conv_taps(start_zero, causal_front(activated), conv_weight, FRAMES)
        decoded = (hidden.astype(jnp.float32) + branch + conv_bias[:, None]).astype(jnp.bfloat16)
        return decoded.reshape(DCH, FRAMES, LH * LW).transpose(1, 0, 2)
    return lax.map(one_video, video_ids)
```

```python
import math

import jax
import jax.numpy as jnp
from jax import lax
from jax.experimental import pallas as pl
from jax.experimental.pallas import tpu as pltpu
from jax.sharding import PartitionSpec as P

HD = 128
TXT = 256
DCH = 512
GROUPS = 32
PW = 16
EPSILON = 1e-06

F32 = jnp.float32
BF16 = jnp.bfloat16
VMEM = pl.BlockSpec(memory_space=pltpu.VMEM)
SMEM = pl.BlockSpec(memory_space=pltpu.SMEM)
PARAMS = pltpu.CompilerParams(vmem_limit_bytes=48 * 1024 * 1024)


def normed_rows(values, row_gain):
    mean_square = jnp.mean(values * values, axis=-1, keepdims=True)
    return values * lax.rsqrt(mean_square + EPSILON) * row_gain


def pack_kernel(place, token_ref, text_ref, query_gain_ref, key_gain_ref, out_ref):
    query_gain = query_gain_ref[...]
    key_gain = key_gain_ref[...]
    token = token_ref[...].astype(F32).reshape(16, 3, 24, HD)
    text = text_ref[...].astype(F32).reshape(8, 2, 24, HD)
    token_rows = [
        jnp.swapaxes(normed_rows(token[:, 0], query_gain), 0, 1).astype(BF16),
        jnp.swapaxes(normed_rows(token[:, 1], key_gain), 0, 1).astype(BF16),
        jnp.swapaxes(token[:, 2], 0, 1).astype(BF16),
    ]
    text_keys = jnp.swapaxes(normed_rows(text[:, 0], key_gain), 0, 1)
    text_values = jnp.swapaxes(text[:, 1], 0, 1)
    text_rows = jnp.concatenate([text_keys, text_values], axis=1).astype(BF16)
    for seq in range(8):
        for head in range(3):
            source = 3 * seq + head
            target = 4 * seq + head
            for slot in range(3):
                out_ref[target, 16 * slot : 16 * slot + 16, :] = token_rows[slot][source]
            out_ref[target, 48:64, :] = text_rows[source]
        out_ref[4 * seq + 3] = jnp.zeros((64, HD), BF16)


def attend_kernel(limits, rows_ref, out_ref):
    keys = jnp.concatenate(
        [
            rows_ref[:, :, 16:32, :].reshape(512, HD),
            rows_ref[:, :, 48:64, :].astype(F32)[:, :, 0:8].reshape(TXT, HD).astype(BF16),
        ],
        axis=0,
    )
    values = jnp.concatenate(
        [
            rows_ref[:, :, 32:48, :].reshape(512, HD),
            rows_ref[:, :, 48:64, :].astype(F32)[:, :, 8:16].reshape(TXT, HD).astype(BF16),
        ],
        axis=0,
    )
    column = lax.broadcasted_iota(jnp.int32, (1, 512 + TXT), 1)
    position = jnp.where(column < 512, (column >> 3) & 7, column - 512)
    limit = jnp.where(column < 512, limits[0], limits[1])
    penalty = jnp.where(position < limit, 0.0, -jnp.inf)
    for frame in range(4):
        queries = rows_ref[:, frame, 0:16, :].reshape(128, HD)
        scores = lax.dot_general(
            queries, keys, (((1,), (1,)), ((), ())), preferred_element_type=F32
        ) * (1.0 / math.sqrt(HD))
        scores = scores + penalty
        weights = jnp.exp(scores - jnp.max(scores, axis=-1, keepdims=True))
        weight_sum = jnp.sum(weights, axis=-1, keepdims=True)
        attended = jnp.dot(weights.astype(BF16), values, preferred_element_type=F32)
        out_ref[frame] = (attended / weight_sum).astype(BF16)


def project_kernel(attended_ref, weight_ref, out_ref):
    attended = jnp.concatenate([attended_ref[0], attended_ref[1], attended_ref[2]], axis=1)
    for start in range(0, 3072, 512):
        weight = weight_ref[:, :, start : start + 512].reshape(3 * HD, 512)
        total = jnp.dot(attended, weight, preferred_element_type=F32)
        out_ref[:, :, start : start + 512] = total.astype(BF16).reshape(8, 16, 512)


def latent_kernel(
    place, parts_ref, residual_ref, gate_ref, shift_ref, scale_ref, weight_ref, bias_ref, out_ref
):
    projected = parts_ref[0].astype(F32)
    for source in range(1, 8):
        projected += parts_ref[source].astype(F32)
    block = residual_ref[...].astype(F32) + gate_ref[...] * projected
    centred = block - jnp.mean(block, axis=-1, keepdims=True)
    variance = jnp.mean(centred * centred, axis=-1, keepdims=True)
    normed = centred * lax.rsqrt(variance + EPSILON)
    modulated = (normed * (1.0 + scale_ref[...]) + shift_ref[...]).astype(BF16)
    latent = lax.dot_general(
        weight_ref[...], modulated, (((1,), (1,)), ((), ())), preferred_element_type=F32
    )
    latent = (latent + bias_ref[...]).astype(BF16)
    token = lax.broadcasted_iota(jnp.int32, (16, 128), 0)
    lane = lax.broadcasted_iota(jnp.int32, (16, 128), 1)
    local = ((lane >> 4) & 1) ^ (place[2] & 1)
    spread = jnp.where(token == local * 8 + ((lane & 15) >> 1), 1.0, 0.0).astype(BF16)
    wide = jnp.dot(latent, spread, preferred_element_type=F32)
    entry = lax.broadcasted_iota(jnp.int32, (64, 128), 0)
    lane = lax.broadcasted_iota(jnp.int32, (64, 128), 1)
    wanted = (lane >> 6) * 4 + ((lane >> 5) & 1) * 2 + (lane & 1)
    wide = jnp.where((entry >> 5) * 4 + (entry & 3) == wanted, wide, 0.0).astype(BF16)
    row = lax.broadcasted_iota(jnp.int32, (16, 64), 0)
    entry = lax.broadcasted_iota(jnp.int32, (16, 64), 1)
    pick = jnp.where(((entry >> 2) & 7) == (row & 7), 1.0, 0.0).astype(BF16)
    copies = jnp.dot(pick, wide, preferred_element_type=F32).astype(BF16)
    for pair in range(32):
        out_ref[16 * pair : 16 * pair + 16, :] = copies


def shifted(field, tap):
    step_y = tap // 3 - 1
    step_x = tap % 3 - 1
    offset = 32 * step_y + step_x
    if offset == 0:
        return field
    moved = pltpu.roll(field, (-offset) % 256, 1)
    pixel = lax.broadcasted_iota(jnp.int32, (1, 256), 1)
    row = (pixel >> 5) + step_y
    col = (pixel & 31) + step_x
    inside = (row >= 0) & (row < 8) & (col >= 0) & (col < 32)
    return jnp.where(inside, moved, 0.0)


def decode_kernel(
    place,
    latent_ref,
    in_weight_ref,
    columns_ref,
    weight_ref,
    bias_ref,
    out_ref,
    latent_scratch,
    taps_ref,
    hidden_ref,
    active_ref,
):
    chan = place[0]
    frame = place[1]
    in_bias = columns_ref[:, 48:49]
    gain = columns_ref[:, 49:50]
    bias = columns_ref[:, 50:51]
    latent_scratch[...] = latent_ref[...].astype(F32).reshape(64, 8, 128)
    lane = lax.broadcasted_iota(jnp.int32, (1, 128), 1)
    low = lane < 64
    even = (lane & 16) == 0
    for video in range(2):
        fields = []
        for step in range(3):
            slab = frame - 2 + step
            held = jnp.maximum(slab, 0)
            frames = ([], [])
            for row in range(4):
                left = latent_scratch[(4 * row + video) * 4 + held]
                right = latent_scratch[(4 * row + 2 + video) * 4 + held]
                frames[0].append(jnp.where(even, left, right))
                crossed = jnp.where(even, right, left)
                crossed = jnp.where(
                    even, pltpu.roll(crossed, 112, 1), pltpu.roll(crossed, 16, 1)
                )
                frames[1].append(crossed)
            made = []
            for rows in frames:
                turned = [pltpu.roll(piece, 64, 1) for piece in rows]
                upper = [jnp.where(low, rows[0], turned[1]), jnp.where(low, rows[2], turned[3])]
                lower = [jnp.where(low, turned[0], rows[1]), jnp.where(low, turned[2], rows[3])]
                made.append(
                    jnp.concatenate(
                        [jnp.concatenate(upper, axis=1), jnp.concatenate(lower, axis=1)], axis=0
                    )
                )
            fields += [made[0], jnp.where(slab < 0, made[0], made[1])]
        stacked = jnp.concatenate(fields, axis=0)
        for tap in range(9):
            moved = shifted(stacked, tap)
            for step in range(6):
                taps_ref[9 * step + tap] = moved[16 * step : 16 * step + 16]
        taps_ref[54:59] = jnp.zeros((5, 16, 256), F32)
        for step in range(4):
            window = taps_ref[9 * step : 9 * step + 32].reshape(DCH, 256).astype(BF16)
            hidden = jnp.dot(in_weight_ref[...], window, preferred_element_type=F32) + in_bias
            hidden = hidden.astype(BF16).astype(F32)
            if step >= 2:
                hidden_ref[step - 2] = hidden.reshape(16, 32, 256)
            halves = hidden[:, :128] + hidden[:, 128:]
            total = jnp.sum(halves.reshape(GROUPS, 16, 128), axis=1)
            mean = jnp.sum(total, axis=1, keepdims=True) * (1.0 / 4096.0)
            square = hidden * hidden
            halves = square[:, :128] + square[:, 128:]
            total = jnp.sum(halves.reshape(GROUPS, 16, 128), axis=1)
            variance = jnp.sum(total, axis=1, keepdims=True) * (1.0 / 4096.0) - mean * mean
            inverse = lax.rsqrt(variance + EPSILON)
            mean = jnp.broadcast_to(mean[:, None, :], (GROUPS, 16, 1)).reshape(DCH, 1)
            inverse = jnp.broadcast_to(inverse[:, None, :], (GROUPS, 16, 1)).reshape(DCH, 1)
            normed = (hidden - mean) * (inverse * gain) + bias
            active = 0.5 * normed * (1.0 + jnp.tanh(0.5 * normed))
            active_ref[step] = active
        for step in range(2):
            branch = jnp.zeros((288, 256), F32)
            for lag in range(3):
                branch += jnp.dot(
                    weight_ref[9 * lag : 9 * lag + 9].reshape(288, DCH),
                    active_ref[step + lag].astype(BF16),
                    preferred_element_type=F32,
                )
            total = hidden_ref[step, chan] + bias_ref[...]
            for tap in range(9):
                total += shifted(branch[32 * tap : 32 * tap + 32], tap)
            out_ref[video, step] = total.astype(BF16)


def on_device(
    token_qkv,
    text_kv,
    residual,
    query_gain,
    key_gain,
    out_weight,
    res_gate,
    mod_shift,
    mod_scale,
    final_weight,
    final_bias,
    text_len,
    video_frames,
    in_weight,
    in_bias,
    group_gain,
    group_bias,
    conv_weight,
    conv_bias,
):
    place = jnp.stack(
        [lax.axis_index("chan"), lax.axis_index("frame"), lax.axis_index("seq")]
    ).astype(jnp.int32)
    limits = jnp.concatenate([video_frames, text_len])

    table = jnp.concatenate(
        [
            in_weight.reshape(432, 32).T.astype(F32),
            in_bias[:, None],
            group_gain[:, None],
            group_bias[:, None],
            jnp.zeros((32, 77), F32),
        ],
        axis=1,
    )
    table = lax.all_gather(table, "chan", axis=0, tiled=True)
    lane = jnp.arange(512)[None]
    in_rows = jnp.where(lane < 432, table, 0.0).astype(BF16)
    columns = table[:, 384:]

    packed = pl.pallas_call(
        pack_kernel,
        out_shape=jax.ShapeDtypeStruct((32, 64, HD), BF16),
        grid_spec=pltpu.PrefetchScalarGridSpec(
            num_scalar_prefetch=1,
            grid=(1,),
            in_specs=[
                pl.BlockSpec((1152, HD), lambda i, p: (0, 0)),
                pl.BlockSpec((384, HD), lambda i, p: (p[1], 0)),
                pl.BlockSpec((1, HD), lambda i, p: (0, 0)),
                pl.BlockSpec((1, HD), lambda i, p: (0, 0)),
            ],
            out_specs=pl.BlockSpec((32, 64, HD), lambda i, p: (0, 0, 0)),
        ),
        compiler_params=pltpu.CompilerParams(vmem_limit_bytes=62 * 1024 * 1024),
        name="pack_rows",
    )(
        place,
        token_qkv.reshape(1152, HD),
        text_kv.reshape(1536, HD),
        query_gain[None],
        key_gain[None],
    )
    rows = lax.all_to_all(packed, ("seq", "frame"), 0, 0, tiled=True)
    attended = pl.pallas_call(
        attend_kernel,
        out_shape=jax.ShapeDtypeStruct((4, 128, HD), BF16),
        in_specs=[SMEM, VMEM],
        out_specs=VMEM,
        compiler_params=PARAMS,
        name="attend",
    )(limits, rows.reshape(8, 4, 64, HD))
    attended = lax.all_to_all(attended, "frame", 0, 0, tiled=True)
    parts = pl.pallas_call(
        project_kernel,
        out_shape=jax.ShapeDtypeStruct((8, 16, 3072), BF16),
        in_specs=[VMEM, VMEM],
        out_specs=VMEM,
        compiler_params=PARAMS,
        name="project",
    )(attended, out_weight)
    parts = lax.all_to_all(parts, "seq", 0, 0, tiled=True)
    latent = pl.pallas_call(
        latent_kernel,
        out_shape=jax.ShapeDtypeStruct((512, 128), BF16),
        in_specs=[SMEM] + [VMEM] * 7,
        out_specs=VMEM,
        compiler_params=PARAMS,
        name="latents",
    )(
        place,
        parts,
        residual.reshape(16, 3072),
        res_gate,
        mod_shift,
        mod_scale,
        final_weight,
        final_bias[:, None],
    )
    latent = lax.all_to_all(latent.reshape(64, 8, 128), ("chan", "frame"), 0, 0, tiled=True)
    latent = lax.all_to_all(latent, "seq", 0, 0, tiled=True)
    return pl.pallas_call(
        decode_kernel,
        out_shape=jax.ShapeDtypeStruct((2, 2, 32, 256), BF16),
        in_specs=[SMEM] + [VMEM] * 5,
        out_specs=VMEM,
        scratch_shapes=[
            pltpu.VMEM((64, 8, 128), F32),
            pltpu.VMEM((59, 16, 256), F32),
            pltpu.VMEM((2, 16, 32, 256), F32),
            pltpu.VMEM((4, DCH, 256), F32),
        ],
        compiler_params=PARAMS,
        name="decode",
    )(
        place,
        latent.reshape(512, 128),
        in_rows,
        columns,
        conv_weight.transpose(0, 2, 1),
        conv_bias[:, None],
    )


def solution(mesh):
    return jax.shard_map(
        on_device,
        mesh=mesh,
        in_specs=(
            P("chan", "frame", "seq", None, None, None),
            P("chan", "seq", None, None, None),
            P("chan", "frame", "seq", None),
            P(),
            P(),
            P("seq", None, None),
            P("chan", None),
            P("chan", None),
            P("chan", None),
            P(),
            P(),
            P("chan"),
            P("chan"),
            P(None, None, "chan"),
            P("chan"),
            P("chan"),
            P("chan"),
            P(None, None, "chan"),
            P("chan"),
        ),
        out_specs=P("seq", "frame", "chan", None),
        check_vma=False,
    )
```

```python
import math

import jax
import jax.numpy as jnp
from jax import lax
from jax.experimental import pallas as pl
from jax.experimental.pallas import tpu as pltpu
from jax.sharding import PartitionSpec as P

HD = 128
TXT = 256
DCH = 512
GROUPS = 32
PW = 16
EPSILON = 1e-06

F32 = jnp.float32
BF16 = jnp.bfloat16
VMEM = pl.BlockSpec(memory_space=pltpu.VMEM)
SMEM = pl.BlockSpec(memory_space=pltpu.SMEM)
PARAMS = pltpu.CompilerParams(vmem_limit_bytes=48 * 1024 * 1024)


def normed_rows(values, row_gain):
    mean_square = jnp.mean(values * values, axis=-1, keepdims=True)
    return values * lax.rsqrt(mean_square + EPSILON) * row_gain


def pack_kernel(token_ref, text_ref, query_gain_ref, key_gain_ref, out_ref):
    query_gain = query_gain_ref[...]
    key_gain = key_gain_ref[...]
    token = token_ref[...].astype(F32).reshape(16, 3, 24, HD)
    text = text_ref[...].astype(F32).reshape(8, 2, 24, HD)
    token_rows = [
        jnp.swapaxes(normed_rows(token[:, 0], query_gain), 0, 1).astype(BF16),
        jnp.swapaxes(normed_rows(token[:, 1], key_gain), 0, 1).astype(BF16),
        jnp.swapaxes(token[:, 2], 0, 1).astype(BF16),
    ]
    text_keys = jnp.swapaxes(normed_rows(text[:, 0], key_gain), 0, 1)
    text_values = jnp.swapaxes(text[:, 1], 0, 1)
    text_rows = jnp.concatenate([text_keys, text_values], axis=1).astype(BF16)
    for seq in range(8):
        for head in range(3):
            source = 3 * seq + head
            target = 4 * seq + head
            for slot in range(3):
                out_ref[target, 16 * slot : 16 * slot + 16, :] = token_rows[slot][source]
            out_ref[target, 48:64, :] = text_rows[source]
        out_ref[4 * seq + 3] = jnp.zeros((64, HD), BF16)


def attend_kernel(limits, rows_ref, out_ref):
    keys = jnp.concatenate(
        [
            rows_ref[:, :, 16:32, :].reshape(512, HD),
            rows_ref[:, :, 48:64, :].astype(F32)[:, :, 0:8].reshape(TXT, HD).astype(BF16),
        ],
        axis=0,
    )
    values = jnp.concatenate(
        [
            rows_ref[:, :, 32:48, :].reshape(512, HD),
            rows_ref[:, :, 48:64, :].astype(F32)[:, :, 8:16].reshape(TXT, HD).astype(BF16),
        ],
        axis=0,
    )
    column = lax.broadcasted_iota(jnp.int32, (1, 512 + TXT), 1)
    position = jnp.where(column < 512, (column >> 3) & 7, column - 512)
    limit = jnp.where(column < 512, limits[0], limits[1])
    penalty = jnp.where(position < limit, 0.0, -jnp.inf)
    for frame in range(4):
        queries = rows_ref[:, frame, 0:16, :].reshape(128, HD)
        scores = lax.dot_general(
            queries, keys, (((1,), (1,)), ((), ())), preferred_element_type=F32
        ) * (1.0 / math.sqrt(HD))
        scores = scores + penalty
        weights = jnp.exp(scores - jnp.max(scores, axis=-1, keepdims=True))
        weight_sum = jnp.sum(weights, axis=-1, keepdims=True)
        attended = jnp.dot(weights.astype(BF16), values, preferred_element_type=F32)
        out_ref[frame] = (attended / weight_sum).astype(BF16)


def project_kernel(attended_ref, weight_ref, out_ref):
    attended = jnp.concatenate([attended_ref[0], attended_ref[1], attended_ref[2]], axis=1)
    for start in range(0, 3072, 512):
        weight = weight_ref[:, :, start : start + 512].reshape(3 * HD, 512)
        total = jnp.dot(attended, weight, preferred_element_type=F32)
        out_ref[:, :, start : start + 512] = total.astype(BF16).reshape(8, 16, 512)


def latent_kernel(
    place, parts_ref, residual_ref, gate_ref, shift_ref, scale_ref, weight_ref, bias_ref, out_ref
):
    projected = parts_ref[0].astype(F32)
    for source in range(1, 8):
        projected += parts_ref[source].astype(F32)
    block = residual_ref[...].astype(F32) + gate_ref[...] * projected
    centred = block - jnp.mean(block, axis=-1, keepdims=True)
    variance = jnp.mean(centred * centred, axis=-1, keepdims=True)
    normed = centred * lax.rsqrt(variance + EPSILON)
    modulated = (normed * (1.0 + scale_ref[...]) + shift_ref[...]).astype(BF16)
    latent = lax.dot_general(
        weight_ref[...], modulated, (((1,), (1,)), ((), ())), preferred_element_type=F32
    )
    latent = (latent + bias_ref[...]).astype(BF16)
    token = lax.broadcasted_iota(jnp.int32, (16, 128), 0)
    lane = lax.broadcasted_iota(jnp.int32, (16, 128), 1)
    local = ((lane >> 4) & 1) ^ (place[2] & 1)
    spread = jnp.where(token == local * 8 + ((lane & 15) >> 1), 1.0, 0.0).astype(BF16)
    wide = jnp.dot(latent, spread, preferred_element_type=F32)
    entry = lax.broadcasted_iota(jnp.int32, (64, 128), 0)
    lane = lax.broadcasted_iota(jnp.int32, (64, 128), 1)
    wanted = (lane >> 6) * 4 + ((lane >> 5) & 1) * 2 + (lane & 1)
    wide = jnp.where((entry >> 5) * 4 + (entry & 3) == wanted, wide, 0.0).astype(BF16)
    row = lax.broadcasted_iota(jnp.int32, (16, 64), 0)
    entry = lax.broadcasted_iota(jnp.int32, (16, 64), 1)
    pick = jnp.where(((entry >> 2) & 7) == (row & 7), 1.0, 0.0).astype(BF16)
    copies = jnp.dot(pick, wide, preferred_element_type=F32).astype(BF16)
    for pair in range(32):
        out_ref[16 * pair : 16 * pair + 16, :] = copies


def shifted(field, tap):
    step_y = tap // 3 - 1
    step_x = tap % 3 - 1
    offset = 32 * step_y + step_x
    if offset == 0:
        return field
    moved = pltpu.roll(field, (-offset) % 256, 1)
    pixel = lax.broadcasted_iota(jnp.int32, (1, 256), 1)
    row = (pixel >> 5) + step_y
    col = (pixel & 31) + step_x
    inside = (row >= 0) & (row < 8) & (col >= 0) & (col < 32)
    return jnp.where(inside, moved, 0.0)


def decode_kernel(
    place,
    latent_ref,
    table_ref,
    weight_ref,
    bias_ref,
    out_ref,
    latent_scratch,
    table_scratch,
    taps_ref,
    hidden_ref,
):
    chan = place[0]
    frame = place[1]
    def position(v):
        return ((v >> 3) & 1) | ((v & 1) << 1) | (v & 4) | ((v & 2) << 2)

    table_scratch[...] = table_ref[...].astype(F32)
    table = jnp.concatenate(
        [table_scratch[position(chan) ^ position(group)] for group in range(16)], axis=0
    )
    in_weight = table[:, :448].astype(BF16)
    gain = 0.5 * (table[:, 435:436] + table[:, 436:437] + table[:, 437:438])
    bias = 0.5 * (table[:, 438:439] + table[:, 439:440] + table[:, 440:441])
    row = lax.broadcasted_iota(jnp.int32, (16, 256), 0)
    ones = jnp.where(row < 3, 1.0, 0.0)
    latent_scratch[...] = latent_ref[...].astype(F32).reshape(64, 8, 128)
    lane = lax.broadcasted_iota(jnp.int32, (1, 128), 1)
    low = lane < 64
    even = (lane & 16) == 0
    for video in range(2):
        fields = []
        for step in range(3):
            slab = frame - 2 + step
            held = jnp.maximum(slab, 0)
            frames = ([], [])
            for row in range(4):
                left = latent_scratch[(4 * row + video) * 4 + held]
                right = latent_scratch[(4 * row + 2 + video) * 4 + held]
                frames[0].append(jnp.where(even, left, right))
                crossed = jnp.where(even, right, left)
                crossed = jnp.where(
                    even, pltpu.roll(crossed, 112, 1), pltpu.roll(crossed, 16, 1)
                )
                frames[1].append(crossed)
            made = []
            for rows in frames:
                turned = [pltpu.roll(piece, 64, 1) for piece in rows]
                upper = [jnp.where(low, rows[0], turned[1]), jnp.where(low, rows[2], turned[3])]
                lower = [jnp.where(low, turned[0], rows[1]), jnp.where(low, turned[2], rows[3])]
                made.append(
                    jnp.concatenate(
                        [jnp.concatenate(upper, axis=1), jnp.concatenate(lower, axis=1)], axis=0
                    )
                )
            fields += [made[0], jnp.where(slab < 0, made[0], made[1])]
        stacked = jnp.concatenate(fields, axis=0)
        for tap in range(9):
            moved = shifted(stacked, tap)
            for step in range(6):
                taps_ref[9 * step + tap] = moved[16 * step : 16 * step + 16]
        active = []
        for step in range(4):
            window = taps_ref[9 * step : 9 * step + 27].reshape(432, 256)
            window = jnp.concatenate([window, ones], axis=0).astype(BF16)
            hidden = jnp.dot(in_weight, window, preferred_element_type=F32)
            hidden = hidden.astype(BF16).astype(F32)
            if step >= 2:
                hidden_ref[step - 2] = hidden.reshape(16, 32, 256)
            halves = hidden[:, :128] + hidden[:, 128:]
            total = jnp.sum(halves.reshape(GROUPS, 16, 128), axis=1)
            mean = jnp.sum(total, axis=1, keepdims=True) * (1.0 / 4096.0)
            square = hidden * hidden
            halves = square[:, :128] + square[:, 128:]
            total = jnp.sum(halves.reshape(GROUPS, 16, 128), axis=1)
            variance = jnp.sum(total, axis=1, keepdims=True) * (1.0 / 4096.0) - mean * mean
            inverse = lax.rsqrt(variance + EPSILON)
            mean = jnp.broadcast_to(mean[:, None, :], (GROUPS, 16, 1)).reshape(DCH, 1)
            inverse = jnp.broadcast_to(inverse[:, None, :], (GROUPS, 16, 1)).reshape(DCH, 1)
            normed = (hidden - mean) * (inverse * gain) + bias
            active.append((normed + normed * jnp.tanh(normed)).astype(BF16))
        for step in range(2):
            branch = jnp.zeros((288, 256), F32)
            for lag in range(3):
                branch += jnp.dot(
                    weight_ref[9 * lag : 9 * lag + 9].reshape(288, DCH),
                    active[step + lag],
                    preferred_element_type=F32,
                )
            total = hidden_ref[step, chan] + bias_ref[...]
            for tap in range(9):
                total += shifted(branch[32 * tap : 32 * tap + 32], tap)
            out_ref[video, step] = total.astype(BF16)


def on_device(
    token_qkv,
    text_kv,
    residual,
    query_gain,
    key_gain,
    out_weight,
    res_gate,
    mod_shift,
    mod_scale,
    final_weight,
    final_bias,
    text_len,
    video_frames,
    in_weight,
    in_bias,
    group_gain,
    group_bias,
    conv_weight,
    conv_bias,
):
    place = jnp.stack(
        [lax.axis_index("chan"), lax.axis_index("frame"), lax.axis_index("seq")]
    ).astype(jnp.int32)
    limits = jnp.concatenate([video_frames, text_len])

    columns = []
    for values in (in_bias, group_gain, group_bias):
        rest = values
        for _ in range(3):
            term = lax.reduce_precision(rest, 8, 7)
            columns.append(term.astype(BF16)[:, None])
            rest = rest - term
    table = jnp.concatenate(
        [in_weight.reshape(432, 32).T] + columns + [jnp.zeros((32, 71), BF16)], axis=1
    )[None]

    def doubled(held, bit):
        other = lax.ppermute(held, "chan", [(i, i ^ bit) for i in range(16)])
        return jnp.concatenate([held, other], axis=0)

    packed = pl.pallas_call(
        pack_kernel,
        out_shape=jax.ShapeDtypeStruct((32, 64, HD), BF16),
        grid=(1,),
        in_specs=[
            pl.BlockSpec((1152, HD), lambda i: (0, 0)),
            pl.BlockSpec((384, HD), lambda i: (lax.axis_index("frame"), 0)),
            pl.BlockSpec((1, HD), lambda i: (0, 0)),
            pl.BlockSpec((1, HD), lambda i: (0, 0)),
        ],
        out_specs=pl.BlockSpec((32, 64, HD), lambda i: (0, 0, 0)),
        compiler_params=pltpu.CompilerParams(vmem_limit_bytes=62 * 1024 * 1024),
        name="pack_rows",
    )(
        token_qkv.reshape(1152, HD),
        text_kv.reshape(1536, HD),
        query_gain[None],
        key_gain[None],
    )
    rows = lax.all_to_all(packed, ("seq", "frame"), 0, 0, tiled=True)
    table = doubled(doubled(table, 8), 1)
    rows, table = lax.optimization_barrier((rows, table))
    attended = pl.pallas_call(
        attend_kernel,
        out_shape=jax.ShapeDtypeStruct((4, 128, HD), BF16),
        in_specs=[SMEM, VMEM],
        out_specs=VMEM,
        compiler_params=PARAMS,
        name="attend",
    )(limits, rows.reshape(8, 4, 64, HD))
    attended = lax.all_to_all(attended, "frame", 0, 0, tiled=True)
    parts = pl.pallas_call(
        project_kernel,
        out_shape=jax.ShapeDtypeStruct((8, 16, 3072), BF16),
        in_specs=[VMEM, VMEM],
        out_specs=VMEM,
        compiler_params=PARAMS,
        name="project",
    )(attended, out_weight)
    parts = lax.all_to_all(parts, "seq", 0, 0, tiled=True)
    table = doubled(doubled(table, 4), 2)
    parts, table = lax.optimization_barrier((parts, table))
    latent = pl.pallas_call(
        latent_kernel,
        out_shape=jax.ShapeDtypeStruct((512, 128), BF16),
        in_specs=[SMEM] + [VMEM] * 7,
        out_specs=VMEM,
        compiler_params=PARAMS,
        name="latents",
    )(
        place,
        parts,
        residual.reshape(16, 3072),
        res_gate,
        mod_shift,
        mod_scale,
        final_weight,
        final_bias[:, None],
    )
    latent = lax.all_to_all(latent.reshape(64, 8, 128), ("chan", "frame"), 0, 0, tiled=True)
    latent = lax.all_to_all(latent, "seq", 0, 0, tiled=True)
    return pl.pallas_call(
        decode_kernel,
        out_shape=jax.ShapeDtypeStruct((2, 2, 32, 256), BF16),
        in_specs=[SMEM] + [VMEM] * 4,
        out_specs=VMEM,
        scratch_shapes=[
            pltpu.VMEM((64, 8, 128), F32),
            pltpu.VMEM((16, 32, DCH), F32),
            pltpu.VMEM((54, 16, 256), F32),
            pltpu.VMEM((2, 16, 32, 256), F32),
        ],
        compiler_params=PARAMS,
        name="decode",
    )(
        place,
        latent.reshape(512, 128),
        table,
        conv_weight.transpose(0, 2, 1),
        conv_bias[:, None],
    )


def solution(mesh):
    return jax.shard_map(
        on_device,
        mesh=mesh,
        in_specs=(
            P("chan", "frame", "seq", None, None, None),
            P("chan", "seq", None, None, None),
            P("chan", "frame", "seq", None),
            P(),
            P(),
            P("seq", None, None),
            P("chan", None),
            P("chan", None),
            P("chan", None),
            P(),
            P(),
            P("chan"),
            P("chan"),
            P(None, None, "chan"),
            P("chan"),
            P("chan"),
            P("chan"),
            P(None, None, "chan"),
            P("chan"),
        ),
        out_specs=P("seq", "frame", "chan", None),
        check_vma=False,
    )
```

```python
import math

import jax
import jax.numpy as jnp
from jax import lax
from jax.experimental import pallas as pl
from jax.experimental.pallas import tpu as pltpu
from jax.sharding import PartitionSpec as P

HD = 128
TXT = 256
DCH = 512
GROUPS = 32
PW = 16
EPSILON = 1e-06

F32 = jnp.float32
BF16 = jnp.bfloat16
VMEM = pl.BlockSpec(memory_space=pltpu.VMEM)
SMEM = pl.BlockSpec(memory_space=pltpu.SMEM)
PARAMS = pltpu.CompilerParams(vmem_limit_bytes=48 * 1024 * 1024)


def normed_rows(values, row_gain):
    mean_square = jnp.mean(values * values, axis=-1, keepdims=True)
    return values * lax.rsqrt(mean_square + EPSILON) * row_gain


def pack_kernel(token_ref, text_ref, query_gain_ref, key_gain_ref, out_ref):
    query_gain = query_gain_ref[...]
    key_gain = key_gain_ref[...]
    token = token_ref[...].astype(F32).reshape(16, 3, 24, HD)
    text = text_ref[...].astype(F32).reshape(8, 2, 24, HD)
    token_rows = [
        jnp.swapaxes(normed_rows(token[:, 0], query_gain), 0, 1).astype(BF16),
        jnp.swapaxes(normed_rows(token[:, 1], key_gain), 0, 1).astype(BF16),
        jnp.swapaxes(token[:, 2], 0, 1).astype(BF16),
    ]
    text_keys = jnp.swapaxes(normed_rows(text[:, 0], key_gain), 0, 1)
    text_values = jnp.swapaxes(text[:, 1], 0, 1)
    text_rows = jnp.concatenate([text_keys, text_values], axis=1).astype(BF16)
    for seq in range(8):
        for head in range(3):
            source = 3 * seq + head
            target = 4 * seq + head
            for slot in range(3):
                out_ref[target, 16 * slot : 16 * slot + 16, :] = token_rows[slot][source]
            out_ref[target, 48:64, :] = text_rows[source]
        out_ref[4 * seq + 3] = jnp.zeros((64, HD), BF16)


def attend_kernel(limits, rows_ref, out_ref):
    keys = jnp.concatenate(
        [
            rows_ref[:, :, 16:32, :].reshape(512, HD),
            rows_ref[:, :, 48:64, :].astype(F32)[:, :, 0:8].reshape(TXT, HD).astype(BF16),
        ],
        axis=0,
    )
    values = jnp.concatenate(
        [
            rows_ref[:, :, 32:48, :].reshape(512, HD),
            rows_ref[:, :, 48:64, :].astype(F32)[:, :, 8:16].reshape(TXT, HD).astype(BF16),
        ],
        axis=0,
    )
    column = lax.broadcasted_iota(jnp.int32, (1, 512 + TXT), 1)
    position = jnp.where(column < 512, (column >> 3) & 7, column - 512)
    limit = jnp.where(column < 512, limits[0], limits[1])
    penalty = jnp.where(position < limit, 0.0, -jnp.inf)
    for frame in range(4):
        queries = rows_ref[:, frame, 0:16, :].reshape(128, HD)
        scores = lax.dot_general(
            queries, keys, (((1,), (1,)), ((), ())), preferred_element_type=F32
        ) * (1.0 / math.sqrt(HD))
        scores = scores + penalty
        weights = jnp.exp(scores - jnp.max(scores, axis=-1, keepdims=True))
        weight_sum = jnp.sum(weights, axis=-1, keepdims=True)
        attended = jnp.dot(weights.astype(BF16), values, preferred_element_type=F32)
        out_ref[frame] = (attended / weight_sum).astype(BF16)


def project_kernel(attended_ref, weight_ref, out_ref):
    attended = jnp.concatenate([attended_ref[0], attended_ref[1], attended_ref[2]], axis=1)
    for start in range(0, 3072, 512):
        weight = weight_ref[:, :, start : start + 512].reshape(3 * HD, 512)
        total = jnp.dot(attended, weight, preferred_element_type=F32)
        out_ref[:, :, start : start + 512] = total.astype(BF16).reshape(8, 16, 512)


def latent_kernel(
    place, parts_ref, residual_ref, gate_ref, shift_ref, scale_ref, weight_ref, bias_ref, out_ref
):
    projected = parts_ref[0].astype(F32)
    for source in range(1, 8):
        projected += parts_ref[source].astype(F32)
    block = residual_ref[...].astype(F32) + gate_ref[...] * projected
    centred = block - jnp.mean(block, axis=-1, keepdims=True)
    variance = jnp.mean(centred * centred, axis=-1, keepdims=True)
    normed = centred * lax.rsqrt(variance + EPSILON)
    modulated = (normed * (1.0 + scale_ref[...]) + shift_ref[...]).astype(BF16)
    latent = lax.dot_general(
        weight_ref[...], modulated, (((1,), (1,)), ((), ())), preferred_element_type=F32
    )
    latent = (latent + bias_ref[...]).astype(BF16)
    token = lax.broadcasted_iota(jnp.int32, (16, 128), 0)
    lane = lax.broadcasted_iota(jnp.int32, (16, 128), 1)
    local = ((lane >> 4) & 1) ^ (place[2] & 1)
    spread = jnp.where(token == local * 8 + ((lane & 15) >> 1), 1.0, 0.0).astype(BF16)
    wide = jnp.dot(latent, spread, preferred_element_type=F32)
    entry = lax.broadcasted_iota(jnp.int32, (64, 128), 0)
    lane = lax.broadcasted_iota(jnp.int32, (64, 128), 1)
    wanted = (lane >> 6) * 4 + ((lane >> 5) & 1) * 2 + (lane & 1)
    wide = jnp.where((entry >> 5) * 4 + (entry & 3) == wanted, wide, 0.0).astype(BF16)
    row = lax.broadcasted_iota(jnp.int32, (16, 64), 0)
    entry = lax.broadcasted_iota(jnp.int32, (16, 64), 1)
    pick = jnp.where(((entry >> 2) & 7) == (row & 7), 1.0, 0.0).astype(BF16)
    copies = jnp.dot(pick, wide, preferred_element_type=F32).astype(BF16)
    for pair in range(32):
        out_ref[16 * pair : 16 * pair + 16, :] = copies


def shifted(field, tap):
    step_y = tap // 3 - 1
    step_x = tap % 3 - 1
    offset = 32 * step_y + step_x
    if offset == 0:
        return field
    moved = pltpu.roll(field, (-offset) % 256, 1)
    pixel = lax.broadcasted_iota(jnp.int32, (1, 256), 1)
    row = (pixel >> 5) + step_y
    col = (pixel & 31) + step_x
    inside = (row >= 0) & (row < 8) & (col >= 0) & (col < 32)
    return jnp.where(inside, moved, 0.0)


def decode_kernel(
    place,
    latent_ref,
    table_ref,
    weight_ref,
    bias_ref,
    out_ref,
    latent_scratch,
    table_scratch,
    taps_ref,
    hidden_ref,
):
    chan = place[0]
    frame = place[1]
    def position(v):
        return ((v >> 3) & 1) | ((v & 4) >> 1) | ((v & 2) << 1) | ((v & 1) << 3)

    table_scratch[...] = table_ref[...].astype(F32)
    table = jnp.concatenate(
        [table_scratch[position(chan) ^ position(group)] for group in range(16)], axis=0
    )
    in_weight = table[:, :448].astype(BF16)
    gain = 0.5 * (table[:, 435:436] + table[:, 436:437] + table[:, 437:438])
    bias = 0.5 * (table[:, 438:439] + table[:, 439:440] + table[:, 440:441])
    row = lax.broadcasted_iota(jnp.int32, (16, 256), 0)
    ones = jnp.where(row < 3, 1.0, 0.0)
    latent_scratch[...] = latent_ref[...].astype(F32).reshape(64, 8, 128)
    lane = lax.broadcasted_iota(jnp.int32, (1, 128), 1)
    low = lane < 64
    even = (lane & 16) == 0
    for video in range(2):
        fields = []
        for step in range(3):
            slab = frame - 2 + step
            held = jnp.maximum(slab, 0)
            frames = ([], [])
            for row in range(4):
                left = latent_scratch[(4 * row + video) * 4 + held]
                right = latent_scratch[(4 * row + 2 + video) * 4 + held]
                frames[0].append(jnp.where(even, left, right))
                crossed = jnp.where(even, right, left)
                crossed = jnp.where(
                    even, pltpu.roll(crossed, 112, 1), pltpu.roll(crossed, 16, 1)
                )
                frames[1].append(crossed)
            made = []
            for rows in frames:
                turned = [pltpu.roll(piece, 64, 1) for piece in rows]
                upper = [jnp.where(low, rows[0], turned[1]), jnp.where(low, rows[2], turned[3])]
                lower = [jnp.where(low, turned[0], rows[1]), jnp.where(low, turned[2], rows[3])]
                made.append(
                    jnp.concatenate(
                        [jnp.concatenate(upper, axis=1), jnp.concatenate(lower, axis=1)], axis=0
                    )
                )
            fields += [made[0], jnp.where(slab < 0, made[0], made[1])]
        stacked = jnp.concatenate(fields, axis=0)
        for tap in range(9):
            moved = shifted(stacked, tap)
            for step in range(6):
                taps_ref[9 * step + tap] = moved[16 * step : 16 * step + 16]
        active = []
        for step in range(4):
            window = taps_ref[9 * step : 9 * step + 27].reshape(432, 256)
            window = jnp.concatenate([window, ones], axis=0).astype(BF16)
            hidden = jnp.dot(in_weight, window, preferred_element_type=F32)
            hidden = hidden.astype(BF16).astype(F32)
            if step >= 2:
                hidden_ref[step - 2] = hidden.reshape(16, 32, 256)
            halves = hidden[:, :128] + hidden[:, 128:]
            total = jnp.sum(halves.reshape(GROUPS, 16, 128), axis=1)
            mean = jnp.sum(total, axis=1, keepdims=True) * (1.0 / 4096.0)
            square = hidden * hidden
            halves = square[:, :128] + square[:, 128:]
            total = jnp.sum(halves.reshape(GROUPS, 16, 128), axis=1)
            variance = jnp.sum(total, axis=1, keepdims=True) * (1.0 / 4096.0) - mean * mean
            inverse = lax.rsqrt(variance + EPSILON)
            mean = jnp.broadcast_to(mean[:, None, :], (GROUPS, 16, 1)).reshape(DCH, 1)
            inverse = jnp.broadcast_to(inverse[:, None, :], (GROUPS, 16, 1)).reshape(DCH, 1)
            normed = (hidden - mean) * (inverse * gain) + bias
            active.append((normed + normed * jnp.tanh(normed)).astype(BF16))
        for step in range(2):
            branch = jnp.zeros((288, 256), F32)
            for lag in range(3):
                branch += jnp.dot(
                    weight_ref[9 * lag : 9 * lag + 9].reshape(288, DCH),
                    active[step + lag],
                    preferred_element_type=F32,
                )
            total = hidden_ref[step, chan] + bias_ref[...]
            for tap in range(9):
                total += shifted(branch[32 * tap : 32 * tap + 32], tap)
            out_ref[video, step] = total.astype(BF16)


def on_device(
    token_qkv,
    text_kv,
    residual,
    query_gain,
    key_gain,
    out_weight,
    res_gate,
    mod_shift,
    mod_scale,
    final_weight,
    final_bias,
    text_len,
    video_frames,
    in_weight,
    in_bias,
    group_gain,
    group_bias,
    conv_weight,
    conv_bias,
):
    place = jnp.stack(
        [lax.axis_index("chan"), lax.axis_index("frame"), lax.axis_index("seq")]
    ).astype(jnp.int32)
    limits = jnp.concatenate([video_frames, text_len])

    columns = []
    for values in (in_bias, group_gain, group_bias):
        rest = values
        for _ in range(3):
            term = lax.reduce_precision(rest, 8, 7)
            columns.append(term.astype(BF16)[:, None])
            rest = rest - term
    table = jnp.concatenate(
        [in_weight.reshape(432, 32).T] + columns + [jnp.zeros((32, 71), BF16)], axis=1
    )[None]

    def doubled(held, bit):
        other = lax.ppermute(held, "chan", [(i, i ^ bit) for i in range(16)])
        return jnp.concatenate([held, other], axis=0)

    packed = pl.pallas_call(
        pack_kernel,
        out_shape=jax.ShapeDtypeStruct((32, 64, HD), BF16),
        grid=(1,),
        in_specs=[
            pl.BlockSpec((1152, HD), lambda i: (0, 0)),
            pl.BlockSpec((384, HD), lambda i: (lax.axis_index("frame"), 0)),
            pl.BlockSpec((1, HD), lambda i: (0, 0)),
            pl.BlockSpec((1, HD), lambda i: (0, 0)),
        ],
        out_specs=pl.BlockSpec((32, 64, HD), lambda i: (0, 0, 0)),
        compiler_params=pltpu.CompilerParams(vmem_limit_bytes=62 * 1024 * 1024),
        name="pack_rows",
    )(
        token_qkv.reshape(1152, HD),
        text_kv.reshape(1536, HD),
        query_gain[None],
        key_gain[None],
    )
    rows = lax.all_to_all(packed, ("seq", "frame"), 0, 0, tiled=True)
    table = doubled(table, 8)
    rows, table = lax.optimization_barrier((rows, table))
    attended = pl.pallas_call(
        attend_kernel,
        out_shape=jax.ShapeDtypeStruct((4, 128, HD), BF16),
        in_specs=[SMEM, VMEM],
        out_specs=VMEM,
        compiler_params=PARAMS,
        name="attend",
    )(limits, rows.reshape(8, 4, 64, HD))
    attended = lax.all_to_all(attended, "frame", 0, 0, tiled=True)
    parts = pl.pallas_call(
        project_kernel,
        out_shape=jax.ShapeDtypeStruct((8, 16, 3072), BF16),
        in_specs=[VMEM, VMEM],
        out_specs=VMEM,
        compiler_params=PARAMS,
        name="project",
    )(attended, out_weight)
    parts = lax.all_to_all(parts, "seq", 0, 0, tiled=True)
    table = doubled(doubled(doubled(table, 4), 2), 1)
    parts, table = lax.optimization_barrier((parts, table))
    latent = pl.pallas_call(
        latent_kernel,
        out_shape=jax.ShapeDtypeStruct((512, 128), BF16),
        in_specs=[SMEM] + [VMEM] * 7,
        out_specs=VMEM,
        compiler_params=PARAMS,
        name="latents",
    )(
        place,
        parts,
        residual.reshape(16, 3072),
        res_gate,
        mod_shift,
        mod_scale,
        final_weight,
        final_bias[:, None],
    )
    latent = lax.all_to_all(latent.reshape(64, 8, 128), ("chan", "frame"), 0, 0, tiled=True)
    latent = lax.all_to_all(latent, "seq", 0, 0, tiled=True)
    return pl.pallas_call(
        decode_kernel,
        out_shape=jax.ShapeDtypeStruct((2, 2, 32, 256), BF16),
        in_specs=[SMEM] + [VMEM] * 4,
        out_specs=VMEM,
        scratch_shapes=[
            pltpu.VMEM((64, 8, 128), F32),
            pltpu.VMEM((16, 32, DCH), F32),
            pltpu.VMEM((54, 16, 256), F32),
            pltpu.VMEM((2, 16, 32, 256), F32),
        ],
        compiler_params=PARAMS,
        name="decode",
    )(
        place,
        latent.reshape(512, 128),
        table,
        conv_weight.transpose(0, 2, 1),
        conv_bias[:, None],
    )


def solution(mesh):
    return jax.shard_map(
        on_device,
        mesh=mesh,
        in_specs=(
            P("chan", "frame", "seq", None, None, None),
            P("chan", "seq", None, None, None),
            P("chan", "frame", "seq", None),
            P(),
            P(),
            P("seq", None, None),
            P("chan", None),
            P("chan", None),
            P("chan", None),
            P(),
            P(),
            P("chan"),
            P("chan"),
            P(None, None, "chan"),
            P("chan"),
            P("chan"),
            P("chan"),
            P(None, None, "chan"),
            P("chan"),
        ),
        out_specs=P("seq", "frame", "chan", None),
        check_vma=False,
    )
```

```python
import math

import jax
import jax.numpy as jnp
from jax import lax
from jax.experimental import pallas as pl
from jax.experimental.pallas import tpu as pltpu
from jax.sharding import PartitionSpec as P

HD = 128
TXT = 256
DCH = 512
GROUPS = 32
PW = 16
EPSILON = 1e-06

F32 = jnp.float32
BF16 = jnp.bfloat16
VMEM = pl.BlockSpec(memory_space=pltpu.VMEM)
SMEM = pl.BlockSpec(memory_space=pltpu.SMEM)
PARAMS = pltpu.CompilerParams(vmem_limit_bytes=48 * 1024 * 1024)


def normed_rows(values, row_gain):
    mean_square = jnp.mean(values * values, axis=-1, keepdims=True)
    return values * lax.rsqrt(mean_square + EPSILON) * row_gain


def pack_kernel(token_ref, text_ref, query_gain_ref, key_gain_ref, out_ref):
    query_gain = query_gain_ref[...]
    key_gain = key_gain_ref[...]
    token = token_ref[...].astype(F32).reshape(16, 3, 24, HD)
    text = text_ref[...].astype(F32).reshape(8, 2, 24, HD)
    token_rows = [
        jnp.swapaxes(normed_rows(token[:, 0], query_gain), 0, 1).astype(BF16),
        jnp.swapaxes(normed_rows(token[:, 1], key_gain), 0, 1).astype(BF16),
        jnp.swapaxes(token[:, 2], 0, 1).astype(BF16),
    ]
    text_keys = jnp.swapaxes(normed_rows(text[:, 0], key_gain), 0, 1)
    text_values = jnp.swapaxes(text[:, 1], 0, 1)
    text_rows = jnp.concatenate([text_keys, text_values], axis=1).astype(BF16)
    for seq in range(8):
        for head in range(3):
            source = 3 * seq + head
            target = 4 * seq + head
            for slot in range(3):
                out_ref[target, 16 * slot : 16 * slot + 16, :] = token_rows[slot][source]
            out_ref[target, 48:64, :] = text_rows[source]
        out_ref[4 * seq + 3] = jnp.zeros((64, HD), BF16)


def attend_kernel(limits, rows_ref, out_ref):
    keys = jnp.concatenate(
        [
            rows_ref[:, :, 16:32, :].reshape(512, HD),
            rows_ref[:, :, 48:64, :].astype(F32)[:, :, 0:8].reshape(TXT, HD).astype(BF16),
        ],
        axis=0,
    )
    values = jnp.concatenate(
        [
            rows_ref[:, :, 32:48, :].reshape(512, HD),
            rows_ref[:, :, 48:64, :].astype(F32)[:, :, 8:16].reshape(TXT, HD).astype(BF16),
        ],
        axis=0,
    )
    column = lax.broadcasted_iota(jnp.int32, (1, 512 + TXT), 1)
    position = jnp.where(column < 512, (column >> 3) & 7, column - 512)
    limit = jnp.where(column < 512, limits[0], limits[1])
    penalty = jnp.where(position < limit, 0.0, -jnp.inf)
    scores = []
    for frame in range(4):
        queries = rows_ref[:, frame, 0:16, :].reshape(128, HD)
        products = lax.dot_general(
            queries, keys, (((1,), (1,)), ((), ())), preferred_element_type=F32
        )
        scores.append(products * (1.0 / math.sqrt(HD)) + penalty)
    weights = []
    sums = []
    for frame in range(4):
        raw = jnp.exp(scores[frame] - jnp.max(scores[frame], axis=-1, keepdims=True))
        sums.append(jnp.sum(raw, axis=-1, keepdims=True))
        weights.append(raw.astype(BF16))
    for frame in range(4):
        attended = jnp.dot(weights[frame], values, preferred_element_type=F32)
        out_ref[frame] = (attended / sums[frame]).astype(BF16)


def project_kernel(attended_ref, weight_ref, out_ref):
    attended = jnp.concatenate([attended_ref[0], attended_ref[1], attended_ref[2]], axis=1)
    for start in range(0, 3072, 512):
        weight = weight_ref[:, :, start : start + 512].reshape(3 * HD, 512)
        total = jnp.dot(attended, weight, preferred_element_type=F32)
        out_ref[:, :, start : start + 512] = total.astype(BF16).reshape(8, 16, 512)


def latent_kernel(
    place, parts_ref, residual_ref, gate_ref, shift_ref, scale_ref, weight_ref, bias_ref, out_ref
):
    projected = parts_ref[0].astype(F32)
    for source in range(1, 8):
        projected += parts_ref[source].astype(F32)
    block = residual_ref[...].astype(F32) + gate_ref[...] * projected
    centred = block - jnp.mean(block, axis=-1, keepdims=True)
    variance = jnp.mean(centred * centred, axis=-1, keepdims=True)
    normed = centred * lax.rsqrt(variance + EPSILON)
    modulated = (normed * (1.0 + scale_ref[...]) + shift_ref[...]).astype(BF16)
    latent = lax.dot_general(
        weight_ref[...], modulated, (((1,), (1,)), ((), ())), preferred_element_type=F32
    )
    latent = (latent + bias_ref[...]).astype(BF16)
    token = lax.broadcasted_iota(jnp.int32, (16, 128), 0)
    lane = lax.broadcasted_iota(jnp.int32, (16, 128), 1)
    local = ((lane >> 4) & 1) ^ (place[2] & 1)
    spread = jnp.where(token == local * 8 + ((lane & 15) >> 1), 1.0, 0.0).astype(BF16)
    wide = jnp.dot(latent, spread, preferred_element_type=F32)
    entry = lax.broadcasted_iota(jnp.int32, (64, 128), 0)
    lane = lax.broadcasted_iota(jnp.int32, (64, 128), 1)
    wanted = (lane >> 6) * 4 + ((lane >> 5) & 1) * 2 + (lane & 1)
    wide = jnp.where((entry >> 5) * 4 + (entry & 3) == wanted, wide, 0.0).astype(BF16)
    row = lax.broadcasted_iota(jnp.int32, (16, 64), 0)
    entry = lax.broadcasted_iota(jnp.int32, (16, 64), 1)
    pick = jnp.where(((entry >> 2) & 7) == (row & 7), 1.0, 0.0).astype(BF16)
    copies = jnp.dot(pick, wide, preferred_element_type=F32).astype(BF16)
    for pair in range(32):
        out_ref[16 * pair : 16 * pair + 16, :] = copies


def shifted(field, tap):
    step_y = tap // 3 - 1
    step_x = tap % 3 - 1
    offset = 32 * step_y + step_x
    if offset == 0:
        return field
    moved = pltpu.roll(field, (-offset) % 256, 1)
    pixel = lax.broadcasted_iota(jnp.int32, (1, 256), 1)
    row = (pixel >> 5) + step_y
    col = (pixel & 31) + step_x
    inside = (row >= 0) & (row < 8) & (col >= 0) & (col < 32)
    return jnp.where(inside, moved, 0.0)


def decode_kernel(
    place,
    latent_ref,
    table_ref,
    weight_ref,
    bias_ref,
    out_ref,
    latent_scratch,
    table_scratch,
    taps_ref,
    hidden_ref,
):
    chan = place[0]
    frame = place[1]
    def position(v):
        return ((v >> 3) & 1) | ((v & 4) >> 1) | ((v & 2) << 1) | ((v & 1) << 3)

    table_scratch[...] = table_ref[...].astype(F32)
    table = jnp.concatenate(
        [table_scratch[position(chan) ^ position(group)] for group in range(16)], axis=0
    )
    in_weight = table[:, :448].astype(BF16)
    gain = 0.5 * (table[:, 435:436] + table[:, 436:437] + table[:, 437:438])
    bias = 0.5 * (table[:, 438:439] + table[:, 439:440] + table[:, 440:441])
    gain = jnp.broadcast_to(gain, (DCH, 128))
    bias = jnp.broadcast_to(bias, (DCH, 128))
    row = lax.broadcasted_iota(jnp.int32, (16, 256), 0)
    ones = jnp.where(row < 3, 1.0, 0.0)
    latent_scratch[...] = latent_ref[...].astype(F32).reshape(64, 8, 128)
    lane = lax.broadcasted_iota(jnp.int32, (1, 128), 1)
    low = lane < 64
    even = (lane & 16) == 0
    activated = []
    for video in range(2):
        fields = []
        for step in range(3):
            slab = frame - 2 + step
            held = jnp.maximum(slab, 0)
            frames = ([], [])
            for row in range(4):
                left = latent_scratch[(4 * row + video) * 4 + held]
                right = latent_scratch[(4 * row + 2 + video) * 4 + held]
                frames[0].append(jnp.where(even, left, right))
                crossed = jnp.where(even, right, left)
                crossed = jnp.where(
                    even, pltpu.roll(crossed, 112, 1), pltpu.roll(crossed, 16, 1)
                )
                frames[1].append(crossed)
            made = []
            for rows in frames:
                turned = [pltpu.roll(piece, 64, 1) for piece in rows]
                upper = [jnp.where(low, rows[0], turned[1]), jnp.where(low, rows[2], turned[3])]
                lower = [jnp.where(low, turned[0], rows[1]), jnp.where(low, turned[2], rows[3])]
                made.append(
                    jnp.concatenate(
                        [jnp.concatenate(upper, axis=1), jnp.concatenate(lower, axis=1)], axis=0
                    )
                )
            fields += [made[0], jnp.where(slab < 0, made[0], made[1])]
        stacked = jnp.concatenate(fields, axis=0)
        for tap in range(9):
            moved = shifted(stacked, tap)
            for step in range(6):
                taps_ref[video, 9 * step + tap] = moved[16 * step : 16 * step + 16]
        active = []
        for step in range(4):
            window = taps_ref[video, 9 * step : 9 * step + 27].reshape(432, 256)
            window = jnp.concatenate([window, ones], axis=0).astype(BF16)
            hidden = jnp.dot(in_weight, window, preferred_element_type=F32)
            hidden = hidden.astype(BF16).astype(F32)
            if step >= 2:
                hidden_ref[video, step - 2] = hidden.reshape(16, 32, 256)
            halves = hidden[:, :128] + hidden[:, 128:]
            total = jnp.sum(halves.reshape(GROUPS, 16, 128), axis=1)
            mean = jnp.sum(total, axis=1, keepdims=True) * (1.0 / 4096.0)
            square = hidden * hidden
            halves = square[:, :128] + square[:, 128:]
            total = jnp.sum(halves.reshape(GROUPS, 16, 128), axis=1)
            variance = jnp.sum(total, axis=1, keepdims=True) * (1.0 / 4096.0) - mean * mean
            inverse = lax.rsqrt(variance + EPSILON)
            mean = jnp.broadcast_to(mean[:, :, None], (GROUPS, 16, 128)).reshape(DCH, 128)
            factor = jnp.broadcast_to(inverse[:, :, None], (GROUPS, 16, 128)).reshape(DCH, 128) * gain
            normed = jnp.concatenate(
                [
                    (hidden[:, :128] - mean) * factor + bias,
                    (hidden[:, 128:] - mean) * factor + bias,
                ],
                axis=1,
            )
            active.append((normed + normed * jnp.tanh(normed)).astype(BF16))
        activated.append(active)
    for video in range(2):
        active = activated[video]
        for step in range(2):
            branch = jnp.zeros((288, 256), F32)
            for lag in range(3):
                branch += jnp.dot(
                    weight_ref[9 * lag : 9 * lag + 9].reshape(288, DCH),
                    active[step + lag],
                    preferred_element_type=F32,
                )
            total = hidden_ref[video, step, chan] + bias_ref[...]
            for tap in range(9):
                total += shifted(branch[32 * tap : 32 * tap + 32], tap)
            out_ref[video, step] = total.astype(BF16)


def on_device(
    token_qkv,
    text_kv,
    residual,
    query_gain,
    key_gain,
    out_weight,
    res_gate,
    mod_shift,
    mod_scale,
    final_weight,
    final_bias,
    text_len,
    video_frames,
    in_weight,
    in_bias,
    group_gain,
    group_bias,
    conv_weight,
    conv_bias,
):
    place = jnp.stack(
        [lax.axis_index("chan"), lax.axis_index("frame"), lax.axis_index("seq")]
    ).astype(jnp.int32)
    limits = jnp.concatenate([video_frames, text_len])

    columns = []
    for values in (in_bias, group_gain, group_bias):
        rest = values
        for _ in range(3):
            term = lax.reduce_precision(rest, 8, 7)
            columns.append(term.astype(BF16)[:, None])
            rest = rest - term
    table = jnp.concatenate(
        [in_weight.reshape(432, 32).T] + columns + [jnp.zeros((32, 71), BF16)], axis=1
    )[None]

    def doubled(held, bit):
        other = lax.ppermute(held, "chan", [(i, i ^ bit) for i in range(16)])
        return jnp.concatenate([held, other], axis=0)

    packed = pl.pallas_call(
        pack_kernel,
        out_shape=jax.ShapeDtypeStruct((32, 64, HD), BF16),
        grid=(1,),
        in_specs=[
            pl.BlockSpec((1152, HD), lambda i: (0, 0)),
            pl.BlockSpec((384, HD), lambda i: (lax.axis_index("frame"), 0)),
            pl.BlockSpec((1, HD), lambda i: (0, 0)),
            pl.BlockSpec((1, HD), lambda i: (0, 0)),
        ],
        out_specs=pl.BlockSpec((32, 64, HD), lambda i: (0, 0, 0)),
        compiler_params=pltpu.CompilerParams(vmem_limit_bytes=62 * 1024 * 1024),
        name="pack_rows",
    )(
        token_qkv.reshape(1152, HD),
        text_kv.reshape(1536, HD),
        query_gain[None],
        key_gain[None],
    )
    rows = lax.all_to_all(packed, ("seq", "frame"), 0, 0, tiled=True)
    table = doubled(table, 8)
    rows, table = lax.optimization_barrier((rows, table))
    attended = pl.pallas_call(
        attend_kernel,
        out_shape=jax.ShapeDtypeStruct((4, 128, HD), BF16),
        in_specs=[SMEM, VMEM],
        out_specs=VMEM,
        compiler_params=PARAMS,
        name="attend",
    )(limits, rows.reshape(8, 4, 64, HD))
    attended = lax.all_to_all(attended, "frame", 0, 0, tiled=True)
    parts = pl.pallas_call(
        project_kernel,
        out_shape=jax.ShapeDtypeStruct((8, 16, 3072), BF16),
        in_specs=[VMEM, VMEM],
        out_specs=VMEM,
        compiler_params=PARAMS,
        name="project",
    )(attended, out_weight)
    parts = lax.all_to_all(parts, "seq", 0, 0, tiled=True)
    table = doubled(doubled(doubled(table, 4), 2), 1)
    parts, table = lax.optimization_barrier((parts, table))
    latent = pl.pallas_call(
        latent_kernel,
        out_shape=jax.ShapeDtypeStruct((512, 128), BF16),
        in_specs=[SMEM] + [VMEM] * 7,
        out_specs=VMEM,
        compiler_params=PARAMS,
        name="latents",
    )(
        place,
        parts,
        residual.reshape(16, 3072),
        res_gate,
        mod_shift,
        mod_scale,
        final_weight,
        final_bias[:, None],
    )
    latent = lax.all_to_all(latent.reshape(64, 8, 128), ("chan", "frame"), 0, 0, tiled=True)
    latent = lax.all_to_all(latent, "seq", 0, 0, tiled=True)
    return pl.pallas_call(
        decode_kernel,
        out_shape=jax.ShapeDtypeStruct((2, 2, 32, 256), BF16),
        in_specs=[SMEM] + [VMEM] * 4,
        out_specs=VMEM,
        scratch_shapes=[
            pltpu.VMEM((64, 8, 128), F32),
            pltpu.VMEM((16, 32, DCH), F32),
            pltpu.VMEM((2, 54, 16, 256), F32),
            pltpu.VMEM((2, 2, 16, 32, 256), F32),
        ],
        compiler_params=PARAMS,
        name="decode",
    )(
        place,
        latent.reshape(512, 128),
        table,
        conv_weight.transpose(0, 2, 1),
        conv_bias[:, None],
    )


def solution(mesh):
    return jax.shard_map(
        on_device,
        mesh=mesh,
        in_specs=(
            P("chan", "frame", "seq", None, None, None),
            P("chan", "seq", None, None, None),
            P("chan", "frame", "seq", None),
            P(),
            P(),
            P("seq", None, None),
            P("chan", None),
            P("chan", None),
            P("chan", None),
            P(),
            P(),
            P("chan"),
            P("chan"),
            P(None, None, "chan"),
            P("chan"),
            P("chan"),
            P("chan"),
            P(None, None, "chan"),
            P("chan"),
        ),
        out_specs=P("seq", "frame", "chan", None),
        check_vma=False,
    )
```
